256 devices in a mesh: dev: 256 (over y, z, x, core).
Axes of the slice: x: 4, y: 4, z: 8, core: 2. Of those that a mesh axis runs over, the one named last changes fastest.
Arguments:
- block_in: float32 [2048, 4096], P('dev'), may hold values from -6 to 6
- leaf_basis: float32 [2048, 2048], P('dev'), may hold values from -0.75 to 0.75
- transfer: float32 [3840, 1024], P('dev'), may hold values from -0.875 to 0.875
- upper_transfer: float32 [252, 1024], replicated, may hold values from -0.875 to 0.875
- near_count: int32 [2048], P('dev'), may hold values from 1 to 12, as said below
- near_partner: int32 [2048, 12], P('dev'), may hold values from 0 to 2047, as said below
- near_block: float32 [2048, 12, 4096], P('dev'), may hold values from -0.3125 to 0.3125
- far_count: int32 [3840], P('dev'), may hold values from 1 to 8, as said below
- far_partner: int32 [3840, 8], P('dev'), may hold values from 0 to 2047, as said below
- coupling: float32 [3840, 8, 1024], P('dev'), may hold values from -0.21875 to 0.21875
- upper_pair: int32 [1024, 2], P('dev'), may hold values from 0 to 253, as said below
- upper_block: float32 [1024, 1024], P('dev'), may hold values from -0.21875 to 0.21875
Outputs:
- first_image: float32 [2048, 4096], P('dev')
- second_image: float32 [2048, 4096], P('dev')
The draws below stay inside these ranges and needn't reach their ends.
Inputs may be any that keep to these rules, and one draw needn't show every extreme that they name: `near_partner`: slot 0 of leaf t's list is t itself; every listed leaf lies within 2 leaves of t. Only the first near_count[t] slots of a leaf's list and blocks count; some leaf uses all of them. `far_partner`: row r of local cluster (j, p) names clusters p2 of level j, p2 != p, with |p2 - p| at most the number of level-j clusters that one device holds. Only the first far_count[r] slots of a cluster's list and couplings count; some cluster uses all of them. `upper_pair`: column 0 is the target and column 1 the source of a block, both in the upper numbering; they lie in the same level and differ.
All inputs are finite; a program needn't handle non-finite values.
Results may differ from the reference program's by a relative error of at most 0.0003.
Values sent between devices are 32-bit elements; how exact they have to be, the bound alone decides.
No kernel may reach another device: no remote copies, remote signals or barrier semaphores. Data moves between devices by JAX's collectives and lax.ppermute only.
A program may use at most 192 MiB of HBM per device.

```python
import jax
import jax.numpy as jnp
import numpy as np
from jax import lax

NRHS = 64
LEAF = 64
RANK = 32
NEARP = 12
FARP = 8
L_DEV = 8
TOPS = 256
NL = 2048
CPD = 15
NLC = 3840
NW = 2
UPC = 254
UPE = 252
NBLK = 1024


def draw_counts(key, length, most):
    key_count, key_fullest = jax.random.split(key)
    counts = jax.random.randint(key_count, (length,), 1, most + 1)
    fullest = jax.random.randint(key_fullest, (), 0, length)
    return counts.at[fullest].set(most).astype(jnp.int32)


def draw_near_count(key, part):
    key = jax.random.fold_in(key, 3)
    return draw_counts(key, NL, NEARP)


def draw_far_count(key, part):
    key = jax.random.fold_in(key, 5)
    return draw_counts(key, NLC, FARP)


def draw_near_partner(key, part):
    key = jax.random.fold_in(key, 7)
    leaves = jnp.arange(NL, dtype=jnp.int32)[:, None]
    offset = jax.random.randint(key, (NL, NEARP), -NW, NW + 1)
    chosen = leaves + offset
    outside = (chosen < 0) | (chosen >= NL)
    chosen = jnp.where(outside, leaves - offset, chosen)
    return chosen.at[:, 0].set(leaves[:, 0]).astype(jnp.int32)


def draw_far_partner(key, part):
    key = jax.random.fold_in(key, 9)
    breadth_list = []
    position_list = []
    for height in range(L_DEV.bit_length()):
        breadth = L_DEV >> height
        breadth_list = breadth_list + [breadth] * breadth
        position_list = position_list + list(range(breadth))
    breadths = np.array(breadth_list * TOPS, np.int32)
    positions = np.array(position_list * TOPS, np.int32)
    device_rows = np.repeat(np.arange(TOPS, dtype=np.int32), CPD)
    cluster = jnp.asarray(device_rows * breadths + positions)[:, None]
    level_total = jnp.asarray(TOPS * breadths)[:, None]
    key_size, key_sign = jax.random.split(key)
    magnitude = jax.random.randint(key_size, (NLC, FARP), 1, jnp.asarray(breadths)[:, None] + 1)
    direction = jax.random.randint(key_sign, (NLC, FARP), 0, 2) * 2 - 1
    stride = magnitude * direction
    chosen = cluster + stride
    outside = (chosen < 0) | (chosen >= level_total)
    chosen = jnp.where(outside, cluster - stride, chosen)
    chosen = chosen.at[1, 0].set(0)
    chosen = chosen.at[(TOPS - 1) * CPD + L_DEV - 2, 0].set(NL - 1)
    return chosen.astype(jnp.int32)


def draw_upper_pair(key, part):
    key = jax.random.fold_in(key, 11)
    size_list = []
    for halving in range(1, TOPS.bit_length() - 1):
        clusters = TOPS >> halving
        size_list = size_list + [clusters] * clusters
    level_table = jnp.asarray(np.array(size_list, np.int32))
    key_target, key_stride = jax.random.split(key)
    target = jax.random.randint(key_target, (NBLK,), 0, UPC)
    target = target.at[0].set(0).at[1].set(UPC - 1)
    clusters = level_table[target]
    offset = TOPS - 2 * clusters
    stride = jax.random.randint(key_stride, (NBLK,), 1, jnp.minimum(clusters - 1, 4) + 1)
    source = offset + (target - offset + stride) % clusters
    return jnp.stack([target, source], axis=1).astype(jnp.int32)


def steps_of(rng, shape, shards, smallest, largest):
    factor_of = 1.0
    for axis_at, parts in shards:
        draws = jax.random.uniform(jax.random.fold_in(jax.random.fold_in(rng, 6), axis_at), (parts,), jnp.float32, smallest / len(shards), largest / len(shards))
        factor_of = factor_of * jnp.repeat(jnp.exp(draws), shape[axis_at] // parts).reshape((-1,) + (1,) * (len(shape) - 1 - axis_at))
    return factor_of


def scatter_about(stream_key, extent, width, bound, cuts=(), held_as=jnp.bfloat16):
    loudness = steps_of(stream_key, extent, cuts, -0.22, 0.18) if cuts else 1.0
    values = jax.random.normal(stream_key, extent, jnp.float32) * width * loudness
    return jnp.minimum(jnp.maximum(values, -bound), bound).astype(held_as)


def setup_inputs(seed: int = 0) -> dict:
    key_list = jax.random.split(jax.random.key(seed), 13)
    block_in = scatter_about(key_list[0], (NL, LEAF * NRHS), 1.0, 6.0, ((0, 256),), jnp.float32)
    leaf_basis = scatter_about(key_list[1], (NL, LEAF * RANK), LEAF ** -0.5, 0.75, ((0, 256),), jnp.float32)
    transfer = scatter_about(key_list[2], (NLC, RANK * RANK), (RANK * 3 // 2) ** -0.5, 0.875, ((0, 256),), jnp.float32)
    upper_transfer = scatter_about(key_list[3], (UPE, RANK * RANK), (RANK * 3 // 2) ** -0.5, 0.875, (), jnp.float32)
    near_count = draw_near_count(jax.random.fold_in(key_list[12], 71), 0)
    near_partner = draw_near_partner(jax.random.fold_in(key_list[12], 71), 0)
    near_block = scatter_about(key_list[6], (NL, NEARP, LEAF * LEAF), (LEAF * NEARP // 2) ** -0.5, 0.3125, ((0, 256),), jnp.float32)
    far_count = draw_far_count(jax.random.fold_in(key_list[12], 71), 0)
    far_partner = draw_far_partner(jax.random.fold_in(key_list[12], 71), 0)
    coupling = scatter_about(key_list[9], (NLC, FARP, RANK * RANK), (RANK * FARP * 3) ** -0.5, 0.21875, ((0, 256),), jnp.float32)
    upper_pair = draw_upper_pair(jax.random.fold_in(key_list[12], 71), 0)
    upper_block = scatter_about(key_list[11], (NBLK, RANK * RANK), (RANK * FARP * 3) ** -0.5, 0.21875, ((0, 256),), jnp.float32)
    return {"block_in": block_in, "leaf_basis": leaf_basis, "transfer": transfer, "upper_transfer": upper_transfer, "near_count": near_count, "near_partner": near_partner, "near_block": near_block, "far_count": far_count, "far_partner": far_partner, "coupling": coupling, "upper_pair": upper_pair, "upper_block": upper_block}


highest = lax.Precision.HIGHEST


def product(form, left, right):
    return jnp.einsum(form, left, right, precision=highest)


def level_rows(height):
    breadth = L_DEV >> height
    return breadth, 2 * L_DEV - 2 * breadth


def per_level(table, height):
    breadth, offset = level_rows(height)
    shaped = table.reshape((TOPS, CPD) + table.shape[1:])
    return shaped[:, offset:offset + breadth].reshape((TOPS * breadth,) + table.shape[1:])


def lift_pairs(weights, coefficients):
    lifted = product('qab,qar->qbr', weights, coefficients)
    return lifted[0::2] + lifted[1::2]


def push_down(weights, coarse, local_terms):
    return local_terms + product('qab,qbr->qar', weights, jnp.repeat(coarse, 2, axis=0))


def far_level(coefficients, count_list, partner_list, block_list):
    clusters = coefficients.shape[0]
    breadth = clusters // TOPS

    def one_block(pieces):
        count_part, partner_part, block_part = pieces
        picked = coefficients[partner_part]
        live_mask = (jnp.arange(FARP)[None, :] < count_part[:, None]).astype(jnp.float32)
        weights = block_part.reshape(breadth, FARP, RANK, RANK) * live_mask[:, :, None, None]
        return product('psab,psbr->par', weights, picked)

    result = lax.map(one_block, (count_list.reshape(TOPS, breadth), partner_list.reshape(TOPS, breadth, FARP), block_list.reshape(TOPS, breadth, FARP, RANK * RANK)))
    return result.reshape(clusters, RANK, NRHS)


def near_term(leaf_rows, near_count, near_partner, near_block):
    def one_block(pieces):
        count_part, partner_part, block_part = pieces
        picked = leaf_rows[partner_part]
        live_mask = (jnp.arange(NEARP)[None, :] < count_part[:, None]).astype(jnp.float32)
        weights = block_part.reshape(L_DEV, NEARP, LEAF, LEAF) * live_mask[:, :, None, None]
        return product('tsij,tsjr->tir', weights, picked)

    result = lax.map(one_block, (near_count.reshape(TOPS, L_DEV), near_partner.reshape(TOPS, L_DEV, NEARP), near_block.reshape(TOPS, L_DEV, NEARP, LEAF * LEAF)))
    return result.reshape(NL, LEAF, NRHS)


def apply_operator(vectors, operands):
    (leaf_basis, transfer, upper_transfer, near_count, near_partner, near_block, far_count, far_partner, coupling, upper_pair, upper_block) = operands
    levels = L_DEV.bit_length()
    leaf_rows = vectors.reshape(NL, LEAF, NRHS)
    leaf_bases = leaf_basis.reshape(NL, LEAF, RANK)
    coefficients = [product('tik,tir->tkr', leaf_bases, leaf_rows)]
    for height in range(1, levels):
        weights = per_level(transfer, height - 1).reshape(-1, RANK, RANK)
        coefficients.append(lift_pairs(weights, coefficients[-1]))
    top_links = per_level(transfer, levels - 1).reshape(TOPS, RANK, RANK)
    level_sizes = [TOPS >> halving for halving in range(1, TOPS.bit_length() - 1)]
    upper_levels = [lift_pairs(top_links, coefficients[-1])]
    for clusters in level_sizes[:-1]:
        offset = TOPS - 2 * clusters
        weights = upper_transfer[offset:offset + clusters].reshape(clusters, RANK, RANK)
        upper_levels.append(lift_pairs(weights, upper_levels[-1]))
    upper_all = jnp.concatenate(upper_levels, axis=0)
    far_terms = [far_level(coefficients[height], per_level(far_count, height), per_level(far_partner, height), per_level(coupling, height)) for height in range(levels)]
    coupled = product('nab,nbr->nar', upper_block.reshape(NBLK, RANK, RANK), upper_all[upper_pair[:, 1]])
    upper_far = jax.ops.segment_sum(coupled, upper_pair[:, 0], num_segments=UPC)
    downward = upper_far[TOPS - 4:TOPS - 2]
    for clusters in reversed(level_sizes[:-1]):
        offset = TOPS - 2 * clusters
        weights = upper_transfer[offset:offset + clusters].reshape(clusters, RANK, RANK)
        downward = push_down(weights, downward, upper_far[offset:offset + clusters])
    downward = push_down(top_links, downward, far_terms[levels - 1])
    for height in range(levels - 1, 0, -1):
        weights = per_level(transfer, height - 1).reshape(-1, RANK, RANK)
        downward = push_down(weights, downward, far_terms[height - 1])
    image_rows = product('tik,tkr->tir', leaf_bases, downward) + near_term(leaf_rows, near_count, near_partner, near_block)
    return image_rows.reshape(NL, LEAF * NRHS)


def reference(block_in, leaf_basis, transfer, upper_transfer, near_count, near_partner, near_block, far_count, far_partner, coupling, upper_pair, upper_block):
    operands = (leaf_basis, transfer, upper_transfer, near_count, near_partner, near_block, far_count, far_partner, coupling, upper_pair, upper_block)
    first_image = apply_operator(block_in, operands)
    second_image = apply_operator(first_image, operands)
    return (first_image, second_image)
```

```python
import jax
import jax.numpy as jnp
import numpy as np
from jax import lax
from jax.experimental import pallas as pl
from jax.experimental.pallas import tpu as pltpu
from jax.sharding import PartitionSpec as P

NRHS = 64
LEAF = 64
RANK = 32
NEARP = 12
FARP = 8
L_DEV = 8
CPD = 15
NW = 2
DEVICES = 256
CHIPS = 128
LEVELS = (128, 64, 32, 16, 8, 4, 2)
UPC = 254
UPE = 252
HOLD = 4
RECORDS = CHIPS * HOLD
ROWS = L_DEV * LEAF
COEF = CPD * RANK
HALF = NRHS // 2
RIM = NW * LEAF
MEMORY = pltpu.CompilerParams(vmem_limit_bytes=56 * 1024 * 1024)

def split(array):
    high = array.astype(jnp.bfloat16)
    return high, (array - high.astype(jnp.float32)).astype(jnp.bfloat16)


def dot(left, right):
    return jnp.dot(left, right, preferred_element_type=jnp.float32)


def mul(left, right):
    lh, ll = split(left)
    rh, rl = split(right)
    return dot(lh, rh) + (dot(lh, rl) + dot(ll, rh))


def first_of(m):
    return DEVICES - 2 * m


def ring(stride, size, step):
    pairs = []
    for i in range(DEVICES):
        at = (i // stride) % size
        pairs.append((i, i + ((at + step) % size - at) * stride))
    return pairs


STAGES = ((8, 2), (16, 4), (64, 4), (2, 4))


def join_kernel(*refs):
    out_ref = refs[-1]
    at = 0
    for ref in refs[:-1]:
        out_ref[at : at + ref.shape[0]] = ref[...]
        at += ref.shape[0]


def join(parts):
    shape = (sum(p.shape[0] for p in parts),) + parts[0].shape[1:]
    return call(join_kernel, [f32(*shape)], parts)[0]


def gather_chips(piece):
    parts = [piece]
    for stride, size in STAGES:
        if len(parts) > 1:
            piece = join(parts)
        parts = [piece] + [
            lax.ppermute(piece, "dev", ring(stride, size, step)) for step in range(1, size)
        ]
    return parts


def gathered_chip(me, place):
    chip = me // 2
    x = (chip - place // 32) & 3
    low = (chip // 4 - place % 2) & 1
    high = (chip // 8 - place // 2 % 4) & 3
    y = (chip // 32 - place // 8 % 4) & 3
    return y * 32 + high * 8 + low * 4 + x


def other_core(array):
    return lax.ppermute(array, "dev", ring(1, 2, 1))


def neighbours(array_up, array_down):
    up = [(i, i + 1) for i in range(DEVICES - 1)]
    down = [(i + 1, i) for i in range(DEVICES - 1)]
    return lax.ppermute(array_up, "dev", up), lax.ppermute(array_down, "dev", down)


def call(kernel, outs, ins, scratch=(), smem=0, flops=1_000_000, size=1_000_000):
    vmem = pl.BlockSpec(memory_space=pltpu.VMEM)
    scalar = pl.BlockSpec(memory_space=pltpu.SMEM)
    return pl.pallas_call(
        kernel,
        out_shape=[jax.ShapeDtypeStruct(s, d) for s, d in outs],
        in_specs=[scalar] * smem + [vmem] * (len(ins) - smem),
        out_specs=[vmem] * len(outs),
        scratch_shapes=list(scratch),
        compiler_params=MEMORY,
        cost_estimate=pl.CostEstimate(flops=flops, bytes_accessed=size, transcendentals=0),
    )(*ins)


def f32(*shape):
    return (shape, jnp.float32)


def pack(matrix):
    return jnp.concatenate([matrix[8 * g : 8 * g + 8] for g in range(4)], axis=1)


def unpack(tile):
    return jnp.concatenate([tile[:, g * RANK : (g + 1) * RANK] for g in range(4)], axis=0)


def pick_half(array, core):
    return jnp.where(core == 0, array[:, :HALF], array[:, HALF:NRHS])


def both_halves(own, other, core):
    return jnp.concatenate(
        [jnp.where(core == 0, own, other), jnp.where(core == 0, other, own)], axis=1
    )


def basis_kernel(v_ref, e_ref, x_ref, low_ref, lowt_ref, top_ref, topt_ref, c_ref, sent_ref):
    bases = [v_ref[...]]
    offset = 0
    breadth = L_DEV
    while breadth >= 1:
        rows = ROWS // breadth
        parts = []
        for p in range(breadth):
            link = e_ref[(offset + p) * RANK : (offset + p + 1) * RANK, :]
            parts.append(mul(bases[-1][p * rows : (p + 1) * rows], link))
        bases.append(jnp.concatenate(parts, axis=0))
        offset += breadth
        breadth //= 2
    blocks = []
    breadth = L_DEV
    for level in bases[:-1]:
        wide = jnp.concatenate([level] * breadth, axis=1)
        row = lax.broadcasted_iota(jnp.int32, wide.shape, 0) // (ROWS // breadth)
        column = lax.broadcasted_iota(jnp.int32, wide.shape, 1) // RANK
        blocks.append(jnp.where(row == column, wide, 0.0))
        breadth //= 2
    whole = jnp.concatenate(blocks + [bases[-1]], axis=1)
    turned = whole.T
    low_ref[...] = whole[:, :COEF]
    top_ref[...] = bases[-1]
    lowt_ref[...] = turned[:COEF]
    topt_ref[...] = turned[COEF:]
    x = x_ref[...]
    everything = mul(turned, jnp.concatenate([x, bases[-1], jnp.zeros((ROWS, 32), jnp.float32)], axis=1))
    c_ref[...] = everything[:COEF, :NRHS]
    sent_ref[...] = everything[COEF:]


def record_kernel(me_ref, own_ref, other_ref, pair_ref, tile_ref, out_ref):
    both = own_ref[...] + other_ref[...]
    out_ref[0, 0:8, :] = pack(pick_half(both, me_ref[0] % 2))
    out_ref[0, 8:16, :] = pair_ref[...]
    out_ref[0, 16:48, :] = tile_ref[...]


def near_kernel(me_ref, count_ref, partner_ref, block_ref, band_ref, total):
    total[...] = jnp.zeros_like(total)
    first = me_ref[0] * L_DEV
    for t in range(L_DEV):
        for s in range(NEARP):

            @pl.when(s < count_ref[t])
            def _(t=t, s=s):
                at = jnp.clip(partner_ref[t, s] - (first + t) + NW, 0, 2 * NW)
                rows = (t * NEARP + s) * LEAF
                total[t, at] += block_ref[rows : rows + LEAF, :]

    for t in range(L_DEV):
        band_ref[t * LEAF : (t + 1) * LEAF, :] = jnp.concatenate(
            [total[t, k] for k in range(2 * NW + 1)], axis=1
        )


def couple_kernel(count_ref, block_ref, out_ref):
    for r in range(CPD):
        parts = []
        for s in range(FARP):
            at = (r * FARP + s) * RANK
            parts.append(jnp.where(s < count_ref[r], block_ref[at : at + RANK, :], 0.0))
        out_ref[r * RANK : (r + 1) * RANK, :] = jnp.concatenate(parts, axis=1)


def local_kernel(
    me_ref, far_ref, band_ref, couple_ref, low_ref, topt_ref, x_ref, c_ref, before_ref, after_ref,
    y_ref, share_ref, xe, ce, far_pick, far_sum
):
    xe[0:RIM, :] = before_ref[COEF:, :]
    xe[RIM : RIM + ROWS, :] = x_ref[...]
    xe[RIM + ROWS :, :] = after_ref[COEF:, :]
    ce[0:COEF, :] = before_ref[:COEF, :]
    ce[COEF : 2 * COEF, :] = c_ref[...]
    ce[2 * COEF :, :] = after_ref[:COEF, :]
    me = me_ref[0]
    r = 0
    breadth = L_DEV
    while breadth >= 1:
        offset = 2 * L_DEV - 2 * breadth
        for _ in range(breadth):
            for s in range(FARP):
                along = jnp.clip(far_ref[r, s] - (me - 1) * breadth, 0, 3 * breadth - 1)
                place = along // breadth * CPD + offset + along % breadth
                at = pl.multiple_of(place * RANK, RANK)
                far_pick[r, s * RANK : (s + 1) * RANK, :] = ce[pl.ds(at, RANK), :]
            r += 1
        breadth //= 2
    for r in range(CPD):
        rows = slice(r * RANK, (r + 1) * RANK)
        far_sum[rows, :] = mul(couple_ref[rows, :], far_pick[r])
    spread = mul(low_ref[...], far_sum[...])
    for t in range(L_DEV):
        rows = slice(t * LEAF, (t + 1) * LEAF)
        window = xe[t * LEAF : (t + 2 * NW + 1) * LEAF, :]
        y_ref[rows, :] = spread[rows] + mul(band_ref[rows, :], window)
    share_ref[...] = mul(topt_ref[...], y_ref[...])


def links_kernel(me_ref, u_ref, q_ref, u3_ref):
    high, low = split(u_ref[...])
    u3_ref[...] = jnp.concatenate([high, low, high], axis=1)
    row = lax.broadcasted_iota(jnp.int32, (128, 128), 0)
    column = lax.broadcasted_iota(jnp.int32, (128, 128), 1)
    same = row // RANK == column // RANK
    product = None
    for k, m in enumerate(LEVELS[:-1]):
        ancestor = first_of(m) + me_ref[0] // (DEVICES // m)
        link = u_ref[pl.ds(pl.multiple_of(ancestor * RANK, RANK), RANK), :]
        product = link if product is None else mul(product, link)
        wide = jnp.concatenate([product.T] * 4, axis=1)
        tall = jnp.concatenate([wide] * 4, axis=0)
        q_ref[k] = jnp.where(same, tall, 0.0)


def fold_kernel(me_ref, p0, p1, p2, p3, q_ref, u3_ref, _, w_ref, t_ref, total, ready, turned):
    pieces = (p0, p1, p2, p3)
    me = me_ref[0]
    per = CHIPS // 4
    for k, piece in enumerate(pieces):
        t_ref[k * per * 8 : (k + 1) * per * 8, :] = piece[:, 0:8, :].reshape(per * 8, 128)
    pairs = jnp.concatenate([piece[:, 8, :] for piece in pieces], axis=0).T
    mask = []
    for j in range(HOLD):
        target = pairs[j : j + 1, :].astype(jnp.int32)
        source = pairs[HOLD + j : HOLD + j + 1, :].astype(jnp.int32)
        wanted = target < 0
        for m in LEVELS:
            wanted = wanted | (target == first_of(m) + me // (DEVICES // m))
        source = jnp.where(wanted, source, -1)
        row = lax.broadcasted_iota(jnp.int32, (256, CHIPS), 0)
        mask.append(jnp.where(row == source, 1.0, 0.0).astype(jnp.bfloat16))
    mask = jnp.concatenate(mask, axis=1)
    for r in range(8):
        rows = jnp.concatenate(
            [piece[:, 16 + 8 * j + r, :] for j in range(HOLD) for piece in pieces], axis=0
        )
        high, low = split(rows)
        both = dot(mask, jnp.concatenate([high, low], axis=1))
        total[:, r, :] = both[:, :128] + both[:, 128:]
    direct = {}
    for k, m in enumerate(LEVELS[1:]):
        o = first_of(m)
        packed = mul(total[o : o + m].reshape(m * 8, 128), q_ref[k])
        for u in range(m):
            direct[m, u] = packed[8 * u : 8 * u + 8]
    above = [unpack(direct[2, u]) for u in range(2)]
    for m in (4, 8, 16, 32, 64, 128):
        o = first_of(m)
        level = []
        for q in range(m // 2):
            high, low = split(above[q])
            stack = jnp.concatenate([high, high, low], axis=0)
            at = (o + 2 * q) * RANK
            grown = dot(u3_ref[at : at + 2 * RANK, :], stack)
            for i in range(2):
                part = grown[i * RANK : (i + 1) * RANK]
                if m < 128:
                    level.append(unpack(direct[m, 2 * q + i]) + part)
                else:
                    ready[2 * q + i] = total[2 * q + i] + pack(part)
        above = level
    for i in range(CHIPS):
        turned[8 * i : 8 * i + 8, :] = ready[gathered_chip(me, i)]
    w_ref[...] = turned[...].T


def diagonal(z):
    return sum(z[g * RANK : (g + 1) * RANK, g * HALF : (g + 1) * HALF] for g in range(4))


def middle_kernel(
    me_ref, w0_ref, w1_ref, t_ref, sent0_ref, sent1_ref, s0_ref, s1_ref, w_ref, ud_ref, next_ref
):
    w = w0_ref[...] + w1_ref[...]
    w_ref[...] = w
    ud = diagonal(mul(w, t_ref[...]))
    ud_ref[...] = ud
    gram = (sent0_ref[...] + sent1_ref[...])[:, NRHS : NRHS + RANK]
    share = pick_half(s0_ref[...] + s1_ref[...], me_ref[0] % 2)
    next_ref[...] = pack(share + mul(gram, ud))


def last_kernel(w_ref, p0, p1, p2, p3, _, ud_ref):
    t = jnp.concatenate([p0[...], p1[...], p2[...], p3[...]], axis=0)
    ud_ref[...] = diagonal(mul(w_ref[...], t))


def finish_up_kernel(me_ref, y_ref, own_ref, other_ref, top_ref, lowt_ref, out_ref, c_ref):
    ud = both_halves(own_ref[...], other_ref[...], me_ref[0] % 2)
    out = y_ref[...] + mul(top_ref[...], ud)
    out_ref[...] = out
    c_ref[...] = mul(lowt_ref[...], out)


def finish_kernel(me_ref, y_ref, own_ref, other_ref, top_ref, out_ref):
    ud = both_halves(own_ref[...], other_ref[...], me_ref[0] % 2)
    out_ref[...] = y_ref[...] + mul(top_ref[...], ud)


def body(
    block_in, leaf_basis, transfer, upper_transfer, near_count, near_partner, near_block,
    far_count, far_partner, coupling, upper_pair, upper_block
):
    me = lax.axis_index("dev").reshape(1)

    vectors = block_in.reshape(ROWS, NRHS)
    low, lowt, top, topt, coefs, sent = call(
        basis_kernel,
        [f32(ROWS, COEF), f32(COEF, ROWS), f32(ROWS, RANK), f32(RANK, ROWS), f32(COEF, NRHS), f32(RANK, 128)],
        [leaf_basis.reshape(ROWS, RANK), transfer.reshape(COEF, RANK), vectors],
        flops=100_000_000,
    )
    sent_other = other_core(sent)

    tiles = upper_block.reshape(HOLD, RANK, 4, 8).transpose(0, 3, 2, 1).reshape(HOLD * 8, 128)
    pairs = jnp.pad(
        upper_pair.astype(jnp.float32).T.reshape(1, 2 * HOLD), ((0, 7), (0, 128 - 2 * HOLD))
    )
    (record,) = call(record_kernel, [f32(1, 48, 128)], [me, sent, sent_other, pairs, tiles], smem=1)
    pieces = gather_chips(record)

    q, links = call(
        links_kernel,
        [f32(6, 128, 128), ((UPE * RANK, 96), jnp.bfloat16)],
        [me, upper_transfer.reshape(UPE * RANK, RANK)],
        smem=1,
    )
    (band,) = call(
        near_kernel,
        [f32(ROWS, (2 * NW + 1) * LEAF)],
        [me, near_count, near_partner, near_block.reshape(L_DEV * NEARP * LEAF, LEAF)],
        scratch=[pltpu.VMEM((L_DEV, 2 * NW + 1, LEAF, LEAF), jnp.float32)],
        smem=3,
    )
    (couple,) = call(
        couple_kernel,
        [f32(COEF, FARP * RANK)],
        [far_count, coupling.reshape(CPD * FARP * RANK, RANK)],
        smem=1,
    )

    def local(x, c):
        before, after = neighbours(
            jnp.concatenate([c, x[ROWS - RIM :]], axis=0), jnp.concatenate([c, x[:RIM]], axis=0)
        )
        return call(
            local_kernel,
            [f32(ROWS, NRHS), f32(RANK, NRHS)],
            [me, far_partner, band, couple, low, topt, x, c, before, after],
            scratch=[
                pltpu.VMEM((ROWS + 2 * RIM, NRHS), jnp.float32),
                pltpu.VMEM((3 * COEF, NRHS), jnp.float32),
                pltpu.VMEM((CPD, FARP * RANK, NRHS), jnp.float32),
                pltpu.VMEM((COEF, NRHS), jnp.float32),
            ],
            smem=2,
            flops=300_000_000,
            size=4_000_000,
        )

    near_first, share = local(vectors, coefs)
    share_other = other_core(share)

    w_own, first_coefs = call(
        fold_kernel,
        [f32(128, CHIPS * 8), f32(CHIPS * 8, 128)],
        [me, *pieces, q, links, share],
        scratch=[
            pltpu.VMEM((256, 8, 128), jnp.float32),
            pltpu.VMEM((CHIPS, 8, 128), jnp.float32),
            pltpu.VMEM((CHIPS * 8, 128), jnp.float32),
        ],
        smem=1,
        flops=100_000_000,
    )
    w, ud, second_record = call(
        middle_kernel,
        [f32(128, CHIPS * 8), f32(RANK, HALF), f32(8, 128)],
        [me, w_own, other_core(w_own), first_coefs, sent, sent_other, share, share_other],
        smem=1,
        flops=100_000_000,
    )
    second_pieces = gather_chips(second_record)

    first_rows, coefs_second = call(
        finish_up_kernel,
        [f32(ROWS, NRHS), f32(COEF, NRHS)],
        [me, near_first, ud, other_core(ud), top, lowt],
        smem=1,
        flops=100_000_000,
    )
    near_second, after = local(first_rows, coefs_second)
    (ud,) = call(last_kernel, [f32(RANK, HALF)], [w, *second_pieces, after], flops=100_000_000)
    (second_rows,) = call(
        finish_kernel, [f32(ROWS, NRHS)], [me, near_second, ud, other_core(ud), top], smem=1
    )
    return (
        first_rows.reshape(L_DEV, LEAF * NRHS),
        second_rows.reshape(L_DEV, LEAF * NRHS),
    )


def solution(mesh):
    in_specs = (
        P("dev", None),
        P("dev", None),
        P("dev", None),
        P(),
        P("dev"),
        P("dev", None),
        P("dev", None, None),
        P("dev"),
        P("dev", None),
        P("dev", None, None),
        P("dev", None),
        P("dev", None),
    )
    out_specs = (P("dev", None), P("dev", None))
    return jax.shard_map(body, mesh=mesh, in_specs=in_specs, out_specs=out_specs, check_vma=False)
```

```python
import jax
import jax.numpy as jnp
import numpy as np
from jax import lax
from jax.experimental import pallas as pl
from jax.experimental.pallas import tpu as pltpu
from jax.sharding import PartitionSpec as P

NRHS = 64
LEAF = 64
RANK = 32
NEARP = 12
FARP = 8
L_DEV = 8
CPD = 15
NW = 2
DEVICES = 256
CHIPS = 128
LEVELS = (128, 64, 32, 16, 8, 4, 2)
UPC = 254
UPE = 252
HOLD = 4
RECORDS = CHIPS * HOLD
ROWS = L_DEV * LEAF
COEF = CPD * RANK
HALF = NRHS // 2
RIM = NW * LEAF
RIM_ROWS = (COEF + RIM) // 2
MIB = 1024 * 1024

def split(array):
    high = array.astype(jnp.bfloat16)
    return high, (array - high.astype(jnp.float32)).astype(jnp.bfloat16)


def dot(left, right):
    return jnp.dot(left, right, preferred_element_type=jnp.float32)


def mul(left, right):
    lh, ll = split(left)
    rh, rl = split(right)
    return dot(lh, rh) + (dot(lh, rl) + dot(ll, rh))


def first_of(m):
    return DEVICES - 2 * m


def ring(stride, size, step):
    pairs = []
    for i in range(DEVICES):
        at = (i // stride) % size
        pairs.append((i, i + ((at + step) % size - at) * stride))
    return pairs


Z_AXIS, Y_AXIS, X_AXIS = (8, 8), (64, 4), (2, 4)
Z_OFFSETS = (0, -1, 1, -3, -4, -2, 3, 2)


def join(parts, after=()):
    whole = jnp.concatenate(parts, axis=0)
    if after:
        whole = lax.optimization_barrier((whole, *after))[0]
    return whole


def spread(piece, axis):
    stride, size = axis
    return [piece] + [
        lax.ppermute(piece, "dev", ring(stride, size, step)) for step in range(1, size)
    ]


def gather_z(piece, after=(), between=()):
    def move(array, step):
        return lax.ppermute(array, "dev", ring(*Z_AXIS, step))

    near = join([piece, move(piece, 1), move(piece, 7)], after=between)
    return join([near, move(near, 3), move(near[:2], 5)], after=after)


def gathered_chip(me, place):
    chip = me // 2
    x = (chip - place // 32) & 3
    z = (chip // 4 + Z_OFFSETS[place % 8]) & 7
    y = (chip // 32 - place // 8 % 4) & 3
    return y * 32 + z * 4 + x


def other_core(array):
    return lax.ppermute(array, "dev", ring(1, 2, 1))


def neighbours(array_up, array_down):
    up = [(i, i + 1) for i in range(DEVICES - 1)]
    down = [(i + 1, i) for i in range(DEVICES - 1)]
    return lax.ppermute(array_up, "dev", up), lax.ppermute(array_down, "dev", down)


def call(kernel, outs, ins, scratch=(), smem=0, flops=1_000_000, size=1_000_000, room=8):
    vmem = pl.BlockSpec(memory_space=pltpu.VMEM)
    scalar = pl.BlockSpec(memory_space=pltpu.SMEM)
    return pl.pallas_call(
        kernel,
        out_shape=[jax.ShapeDtypeStruct(s, d) for s, d in outs],
        in_specs=[scalar] * smem + [vmem] * (len(ins) - smem),
        out_specs=[vmem] * len(outs),
        scratch_shapes=list(scratch),
        compiler_params=pltpu.CompilerParams(vmem_limit_bytes=room * MIB),
        cost_estimate=pl.CostEstimate(flops=flops, bytes_accessed=size, transcendentals=0),
    )(*ins)


def f32(*shape):
    return (shape, jnp.float32)


def pack(matrix):
    return jnp.concatenate([matrix[8 * g : 8 * g + 8] for g in range(4)], axis=1)


def unpack(tile):
    return jnp.concatenate([tile[:, g * RANK : (g + 1) * RANK] for g in range(4)], axis=0)


def pick_half(array, core):
    return jnp.where(core == 0, array[:, :HALF], array[:, HALF:NRHS])


def both_halves(own, other, core):
    return jnp.concatenate(
        [jnp.where(core == 0, own, other), jnp.where(core == 0, other, own)], axis=1
    )


def write_rim(ref, coefs, rows):
    for ref_rows, part in (((0, COEF // 2), coefs), ((COEF // 2, RIM_ROWS), rows)):
        half = part.shape[0] // 2
        ref[ref_rows[0] : ref_rows[1], :] = jnp.concatenate([part[:half], part[half:]], axis=1)


def read_rim(ref, begin, count):
    part = ref[begin : begin + count, :]
    return jnp.concatenate([part[:, :NRHS], part[:, NRHS:]], axis=0)


def read_coefs(ref):
    return read_rim(ref, 0, COEF // 2)


def read_rows(ref):
    return read_rim(ref, COEF // 2, RIM // 2)


def basis_kernel(v_ref, e_ref, x_ref, bb_ref, up_ref, down_ref):
    bases = [v_ref[...]]
    offset = 0
    breadth = L_DEV
    while breadth >= 1:
        rows = ROWS // breadth
        parts = []
        for p in range(breadth):
            link = e_ref[(offset + p) * RANK : (offset + p + 1) * RANK, :]
            parts.append(mul(bases[-1][p * rows : (p + 1) * rows], link))
        bases.append(jnp.concatenate(parts, axis=0))
        offset += breadth
        breadth //= 2
    blocks = []
    breadth = L_DEV
    for level in bases[:-1]:
        wide = jnp.concatenate([level] * breadth, axis=1)
        row = lax.broadcasted_iota(jnp.int32, wide.shape, 0) // (ROWS // breadth)
        column = lax.broadcasted_iota(jnp.int32, wide.shape, 1) // RANK
        blocks.append(jnp.where(row == column, wide, 0.0))
        breadth //= 2
    whole = jnp.concatenate(blocks + [bases[-1]], axis=1)
    turned = whole.T
    bb_ref[:, :ROWS] = whole
    bb_ref[:, ROWS:] = turned
    x = x_ref[...]
    everything = mul(
        turned, jnp.concatenate([x, bases[-1], jnp.zeros((ROWS, 32), jnp.float32)], axis=1)
    )
    write_rim(up_ref, everything[:COEF, :NRHS], x[ROWS - RIM :])
    write_rim(down_ref, everything[:COEF, :NRHS], x[:RIM])
    up_ref[RIM_ROWS:, :] = everything[COEF:]
    down_ref[RIM_ROWS:, :] = everything[COEF:]


def record_kernel(me_ref, own_ref, before_ref, after_ref, pair_ref, tile_ref, out_ref, gram_ref):
    core = me_ref[0] % 2
    other = jnp.where(core == 0, after_ref[RIM_ROWS:, :], before_ref[RIM_ROWS:, :])
    both = own_ref[RIM_ROWS:, :] + other
    out_ref[0, 0:8, :] = pack(pick_half(both, core))
    out_ref[0, 8:16, :] = pair_ref[...]
    out_ref[0, 16:48, :] = tile_ref[...]
    gram_ref[...] = both[:, NRHS : NRHS + RANK]


def near_kernel(me_ref, count_ref, partner_ref, block_ref, band_ref, total):
    total[...] = jnp.zeros_like(total)
    first = me_ref[0] * L_DEV
    for t in range(L_DEV):
        for s in range(NEARP):

            @pl.when(s < count_ref[t])
            def _(t=t, s=s):
                at = jnp.clip(partner_ref[t, s] - (first + t) + NW, 0, 2 * NW)
                rows = (s * L_DEV + t) * LEAF
                total[t, at] += block_ref[rows : rows + LEAF, :]

    for t in range(L_DEV):
        band_ref[t * LEAF : (t + 1) * LEAF, :] = jnp.concatenate(
            [total[t, k] for k in range(2 * NW + 1)], axis=1
        )


def couple_kernel(count_ref, block_ref, out_ref):
    for r in range(CPD):
        parts = []
        for s in range(FARP):
            at = (r * FARP + s) * RANK
            parts.append(jnp.where(s < count_ref[r], block_ref[at : at + RANK, :], 0.0))
        out_ref[r * RANK : (r + 1) * RANK, :] = jnp.concatenate(parts, axis=1)


def local_kernel(
    me_ref, far_ref, band_ref, couple_ref, bb_ref, x_ref, up_ref, before_ref, after_ref,
    y_ref, share_ref, xe, ce, far_pick, far_sum
):
    xe[0:RIM, :] = read_rows(before_ref)
    xe[RIM : RIM + ROWS, :] = x_ref[...]
    xe[RIM + ROWS :, :] = read_rows(after_ref)
    ce[0:COEF, :] = read_coefs(before_ref)
    ce[COEF : 2 * COEF, :] = read_coefs(up_ref)
    ce[2 * COEF :, :] = read_coefs(after_ref)
    me = me_ref[0]
    r = 0
    breadth = L_DEV
    while breadth >= 1:
        offset = 2 * L_DEV - 2 * breadth
        for _ in range(breadth):
            for s in range(FARP):
                along = jnp.clip(far_ref[s, r] - (me - 1) * breadth, 0, 3 * breadth - 1)
                place = along // breadth * CPD + offset + along % breadth
                at = pl.multiple_of(place * RANK, RANK)
                far_pick[r, s * RANK : (s + 1) * RANK, :] = ce[pl.ds(at, RANK), :]
            r += 1
        breadth //= 2
    for r in range(CPD):
        rows = slice(r * RANK, (r + 1) * RANK)
        far_sum[rows, :] = mul(couple_ref[rows, :], far_pick[r])
    spread = mul(bb_ref[:, :COEF], far_sum[...])
    for t in range(L_DEV):
        rows = slice(t * LEAF, (t + 1) * LEAF)
        window = xe[t * LEAF : (t + 2 * NW + 1) * LEAF, :]
        y_ref[rows, :] = spread[rows] + mul(band_ref[rows, :], window)
    share_ref[...] = mul(bb_ref[COEF:, ROWS:], y_ref[...])


def links_kernel(me_ref, u_ref, q_ref):
    row = lax.broadcasted_iota(jnp.int32, (128, 128), 0)
    column = lax.broadcasted_iota(jnp.int32, (128, 128), 1)
    same = row // RANK == column // RANK
    product = None
    for k, m in enumerate(LEVELS[:-1]):
        ancestor = first_of(m) + me_ref[0] // (DEVICES // m)
        link = u_ref[pl.ds(pl.multiple_of(ancestor * RANK, RANK), RANK), :]
        product = link if product is None else mul(product, link)
        wide = jnp.concatenate([product.T] * 4, axis=1)
        tall = jnp.concatenate([wide] * 4, axis=0)
        q_ref[k] = jnp.where(same, tall, 0.0)


def fold_kernel(
    me_ref, a0, a1, a2, a3, b0, b1, b2, b3, q_ref, u_ref, _, w_ref, t_ref, total, ready, turned
):
    first, second = (a0, a1, a2, a3), (b0, b1, b2, b3)
    me = me_ref[0]
    per = CHIPS // 4
    for k, piece in enumerate(first):
        t_ref[k * per * 8 : (k + 1) * per * 8, :] = piece[:, 0:8, :].reshape(per * 8, 128)
    pairs = jnp.concatenate([piece[:, 8, :] for piece in first], axis=0)
    swapped = jnp.concatenate(
        [pairs[per * x + 8 * y : per * x + 8 * y + 8] for y in range(4) for x in range(4)], axis=0
    )
    pairs, swapped = pairs.T, swapped.T
    mask = []
    for j in range(HOLD):
        table = pairs if j == 0 else swapped
        target = table[j : j + 1, :].astype(jnp.int32)
        source = table[HOLD + j : HOLD + j + 1, :].astype(jnp.int32)
        wanted = target < 0
        for m in LEVELS:
            wanted = wanted | (target == first_of(m) + me // (DEVICES // m))
        source = jnp.where(wanted, source, -1)
        row = lax.broadcasted_iota(jnp.int32, (256, CHIPS), 0)
        mask.append(jnp.where(row == source, 1.0, 0.0).astype(jnp.bfloat16))
    mask = jnp.concatenate(mask, axis=1)
    for r in range(8):
        rows = jnp.concatenate(
            [piece[:, 16 + r, :] for piece in first]
            + [piece[:, 8 * j + r, :] for j in range(HOLD - 1) for piece in second],
            axis=0,
        )
        high, low = split(rows)
        both = dot(mask, jnp.concatenate([high, low], axis=1))
        total[:, r, :] = both[:, :128] + both[:, 128:]
    direct = {}
    for k, m in enumerate(LEVELS[1:]):
        o = first_of(m)
        packed = mul(total[o : o + m].reshape(m * 8, 128), q_ref[k])
        for u in range(m):
            direct[m, u] = packed[8 * u : 8 * u + 8]
    above = [unpack(direct[2, u]) for u in range(2)]
    for m in (4, 8, 16, 32, 64, 128):
        o = first_of(m)
        level = []
        for q in range(m // 2):
            high, low = split(above[q])
            stack = jnp.concatenate([high, high, low], axis=0)
            at = (o + 2 * q) * RANK
            left, rest = split(u_ref[at : at + 2 * RANK, :])
            grown = dot(jnp.concatenate([left, rest, left], axis=1), stack)
            for i in range(2):
                part = grown[i * RANK : (i + 1) * RANK]
                if m < 128:
                    level.append(unpack(direct[m, 2 * q + i]) + part)
                else:
                    ready[2 * q + i] = total[2 * q + i] + pack(part)
        above = level
    for i in range(CHIPS):
        turned[8 * i : 8 * i + 8, :] = ready[gathered_chip(me, i)]
    w_ref[...] = turned[...].T


def diagonal(z):
    return sum(z[g * RANK : (g + 1) * RANK, g * HALF : (g + 1) * HALF] for g in range(4))


def middle_kernel(me_ref, w0_ref, w1_ref, t_ref, gram_ref, s0_ref, s1_ref, w_ref, ud_ref, next_ref):
    w = w0_ref[...] + w1_ref[...]
    w_ref[...] = w
    ud = diagonal(mul(w, t_ref[...]))
    ud_ref[...] = ud
    share = pick_half(s0_ref[...] + s1_ref[...], me_ref[0] % 2)
    next_ref[0] = pack(share + mul(gram_ref[...], ud))


def last_kernel(w_ref, p0, p1, p2, p3, _, ud_ref):
    t = jnp.concatenate([p[...].reshape(CHIPS * 2, 128) for p in (p0, p1, p2, p3)], axis=0)
    ud_ref[...] = diagonal(mul(w_ref[...], t))


def finish_up_kernel(me_ref, y_ref, own_ref, other_ref, bb_ref, out_ref, up_ref, down_ref):
    ud = both_halves(own_ref[...], other_ref[...], me_ref[0] % 2)
    out = y_ref[...] + mul(bb_ref[:, COEF:ROWS], ud)
    out_ref[...] = out
    coefs = mul(bb_ref[:COEF, ROWS:], out)
    write_rim(up_ref, coefs, out[ROWS - RIM :])
    write_rim(down_ref, coefs, out[:RIM])


def finish_kernel(me_ref, y_ref, own_ref, other_ref, bb_ref, out_ref):
    ud = both_halves(own_ref[...], other_ref[...], me_ref[0] % 2)
    out_ref[...] = y_ref[...] + mul(bb_ref[:, COEF:ROWS], ud)


def body(
    block_in, leaf_basis, transfer, upper_transfer, near_count, near_partner, near_block,
    far_count, far_partner, coupling, upper_pair, upper_block
):
    me = lax.axis_index("dev").reshape(1)

    vectors = block_in.reshape(ROWS, NRHS)
    bb, up, down = call(
        basis_kernel,
        [f32(ROWS, 2 * ROWS), f32(RIM_ROWS + RANK, 128), f32(RIM_ROWS + RANK, 128)],
        [leaf_basis.reshape(ROWS, RANK), transfer.reshape(COEF, RANK), vectors],
        flops=100_000_000,
    )
    before, after = neighbours(up, down)

    tiles = upper_block.reshape(HOLD, RANK, 4, 8).transpose(0, 3, 2, 1).reshape(HOLD * 8, 128)
    pairs = jnp.pad(
        upper_pair.astype(jnp.float32).T.reshape(1, 2 * HOLD), ((0, 7), (0, 128 - 2 * HOLD))
    )
    record, gram = call(
        record_kernel,
        [f32(1, 48, 128), f32(RANK, RANK)],
        [me, up, before, after, pairs, tiles],
        smem=1,
    )

    (couple,) = call(
        couple_kernel,
        [f32(COEF, FARP * RANK)],
        [far_count, coupling.reshape(CPD * FARP * RANK, RANK)],
        smem=1,
    )
    links = upper_transfer.reshape(UPE * RANK, RANK)
    (q,) = call(links_kernel, [f32(6, 128, 128)], [me, links], smem=1)
    record = gather_z(record, between=[couple], after=[q])

    def local(x, up, before, after):
        return call(
            local_kernel,
            [f32(ROWS, NRHS), f32(RANK, NRHS)],
            [me, far_partner.T, band, couple, bb, x, up, before, after],
            scratch=[
                pltpu.VMEM((ROWS + 2 * RIM, NRHS), jnp.float32),
                pltpu.VMEM((3 * COEF, NRHS), jnp.float32),
                pltpu.VMEM((CPD, FARP * RANK, NRHS), jnp.float32),
                pltpu.VMEM((COEF, NRHS), jnp.float32),
            ],
            smem=2,
            flops=300_000_000,
            size=4_000_000,
        )

    half_a = join(spread(record[:, :24], Y_AXIS))
    half_b = join(spread(record[:, 24:], X_AXIS))
    half_a, half_b, near_block = lax.optimization_barrier(
        (half_a, half_b, near_block.transpose(1, 0, 2))
    )
    pieces = spread(half_a, X_AXIS) + spread(half_b, Y_AXIS)
    (band,) = call(
        near_kernel,
        [f32(ROWS, (2 * NW + 1) * LEAF)],
        [me, near_count, near_partner, near_block.reshape(NEARP * L_DEV * LEAF, LEAF)],
        scratch=[pltpu.VMEM((L_DEV, 2 * NW + 1, LEAF, LEAF), jnp.float32)],
        smem=3,
    )
    near_first, share = local(vectors, up, before, after)
    share_other = other_core(share)

    w_own, first_coefs = call(
        fold_kernel,
        [f32(128, CHIPS * 8), f32(CHIPS * 8, 128)],
        [me, *pieces, q, links, share],
        scratch=[
            pltpu.VMEM((256, 8, 128), jnp.float32),
            pltpu.VMEM((CHIPS, 8, 128), jnp.float32),
            pltpu.VMEM((CHIPS * 8, 128), jnp.float32),
        ],
        smem=1,
        flops=100_000_000,
        room=16,
    )
    w, ud, second_record = call(
        middle_kernel,
        [f32(128, CHIPS * 8), f32(RANK, HALF), f32(1, 8, 128)],
        [me, w_own, other_core(w_own), first_coefs, gram, share, share_other],
        smem=1,
        flops=100_000_000,
    )
    ud_other = other_core(ud)
    first_rows, up, down = call(
        finish_up_kernel,
        [f32(ROWS, NRHS), f32(RIM_ROWS, 128), f32(RIM_ROWS, 128)],
        [me, near_first, ud, ud_other, bb],
        smem=1,
        flops=100_000_000,
    )
    second_record = gather_z(second_record, between=[ud_other], after=[up])
    up, down, second_record = lax.optimization_barrier((up, down, second_record))
    before, after = neighbours(up, down)
    second_pieces = spread(join(spread(second_record, Y_AXIS)), X_AXIS)
    near_second, share = local(first_rows, up, before, after)
    (ud,) = call(last_kernel, [f32(RANK, HALF)], [w, *second_pieces, share], flops=100_000_000)
    (second_rows,) = call(
        finish_kernel, [f32(ROWS, NRHS)], [me, near_second, ud, other_core(ud), bb], smem=1
    )
    return (
        first_rows.reshape(L_DEV, LEAF * NRHS),
        second_rows.reshape(L_DEV, LEAF * NRHS),
    )


def solution(mesh):
    in_specs = (
        P("dev", None),
        P("dev", None),
        P("dev", None),
        P(),
        P("dev"),
        P("dev", None),
        P("dev", None, None),
        P("dev"),
        P("dev", None),
        P("dev", None, None),
        P("dev", None),
        P("dev", None),
    )
    out_specs = (P("dev", None), P("dev", None))
    return jax.shard_map(body, mesh=mesh, in_specs=in_specs, out_specs=out_specs, check_vma=False)
```

```python
import jax
import jax.numpy as jnp
import numpy as np
from jax import lax
from jax.experimental import pallas as pl
from jax.experimental.pallas import tpu as pltpu
from jax.sharding import PartitionSpec as P

NRHS = 64
LEAF = 64
RANK = 32
NEARP = 12
FARP = 8
L_DEV = 8
CPD = 15
NW = 2
DEVICES = 256
CHIPS = 128
LEVELS = (128, 64, 32, 16, 8, 4, 2)
UPC = 254
UPE = 252
HOLD = 4
RECORDS = CHIPS * HOLD
ROWS = L_DEV * LEAF
COEF = CPD * RANK
HALF = NRHS // 2
RIM = NW * LEAF
RIM_ROWS = (COEF + RIM) // 2
MIB = 1024 * 1024

def split(array):
    high = array.astype(jnp.bfloat16)
    return high, (array - high.astype(jnp.float32)).astype(jnp.bfloat16)


def dot(left, right):
    return jnp.dot(left, right, preferred_element_type=jnp.float32)


def mul(left, right):
    lh, ll = split(left)
    rh, rl = split(right)
    return dot(lh, rh) + (dot(lh, rl) + dot(ll, rh))


def first_of(m):
    return DEVICES - 2 * m


def ring(stride, size, step):
    pairs = []
    for i in range(DEVICES):
        at = (i // stride) % size
        pairs.append((i, i + ((at + step) % size - at) * stride))
    return pairs


Z_AXIS, Y_AXIS, X_AXIS = (8, 8), (64, 4), (2, 4)
Z_OFFSETS = (0, -1, 1, -3, -4, -2, 3, 2)


def join(parts, after=()):
    whole = jnp.concatenate(parts, axis=0)
    if after:
        whole = lax.optimization_barrier((whole, *after))[0]
    return whole


def spread(piece, axis):
    stride, size = axis
    return [piece] + [
        lax.ppermute(piece, "dev", ring(stride, size, step)) for step in range(1, size)
    ]


def gather_z(piece, after=(), between=()):
    def move(array, step):
        return lax.ppermute(array, "dev", ring(*Z_AXIS, step))

    near = join([piece, move(piece, 1), move(piece, 7)], after=between)
    return join([near, move(near, 3), move(near[:2], 5)], after=after)


def gathered_chip(me, place):
    chip = me // 2
    x = (chip - place // 32) & 3
    z = (chip // 4 + Z_OFFSETS[place % 8]) & 7
    y = (chip // 32 - place // 8 % 4) & 3
    return y * 32 + z * 4 + x


def other_core(array):
    return lax.ppermute(array, "dev", ring(1, 2, 1))


def neighbours(array_up, array_down):
    up = [(i, i + 1) for i in range(DEVICES - 1)]
    down = [(i + 1, i) for i in range(DEVICES - 1)]
    return lax.ppermute(array_up, "dev", up), lax.ppermute(array_down, "dev", down)


def call(kernel, outs, ins, scratch=(), smem=0, flops=1_000_000, size=1_000_000, room=8):
    vmem = pl.BlockSpec(memory_space=pltpu.VMEM)
    scalar = pl.BlockSpec(memory_space=pltpu.SMEM)
    return pl.pallas_call(
        kernel,
        out_shape=[jax.ShapeDtypeStruct(s, d) for s, d in outs],
        in_specs=[scalar] * smem + [vmem] * (len(ins) - smem),
        out_specs=[vmem] * len(outs),
        scratch_shapes=list(scratch),
        compiler_params=pltpu.CompilerParams(vmem_limit_bytes=room * MIB),
        cost_estimate=pl.CostEstimate(flops=flops, bytes_accessed=size, transcendentals=0),
    )(*ins)


def f32(*shape):
    return (shape, jnp.float32)


def pack(matrix):
    return jnp.concatenate([matrix[8 * g : 8 * g + 8] for g in range(4)], axis=1)


def unpack(tile):
    return jnp.concatenate([tile[:, g * RANK : (g + 1) * RANK] for g in range(4)], axis=0)


def pick_half(array, core):
    return jnp.where(core == 0, array[:, :HALF], array[:, HALF:NRHS])


def both_halves(own, other, core):
    return jnp.concatenate(
        [jnp.where(core == 0, own, other), jnp.where(core == 0, other, own)], axis=1
    )


def write_rim(ref, coefs, rows):
    for ref_rows, part in (((0, COEF // 2), coefs), ((COEF // 2, RIM_ROWS), rows)):
        half = part.shape[0] // 2
        ref[ref_rows[0] : ref_rows[1], :] = jnp.concatenate([part[:half], part[half:]], axis=1)


def read_rim(ref, begin, count):
    part = ref[begin : begin + count, :]
    return jnp.concatenate([part[:, :NRHS], part[:, NRHS:]], axis=0)


def read_coefs(ref):
    return read_rim(ref, 0, COEF // 2)


def read_rows(ref):
    return read_rim(ref, COEF // 2, RIM // 2)


def basis_kernel(v_ref, e_ref, x_ref, bb_ref, up_ref, down_ref):
    bases = [v_ref[...]]
    offset = 0
    breadth = L_DEV
    while breadth >= 1:
        rows = ROWS // breadth
        parts = []
        for p in range(breadth):
            link = e_ref[(offset + p) * RANK : (offset + p + 1) * RANK, :]
            parts.append(mul(bases[-1][p * rows : (p + 1) * rows], link))
        bases.append(jnp.concatenate(parts, axis=0))
        offset += breadth
        breadth //= 2
    blocks = []
    breadth = L_DEV
    for level in bases[:-1]:
        wide = jnp.concatenate([level] * breadth, axis=1)
        row = lax.broadcasted_iota(jnp.int32, wide.shape, 0) // (ROWS // breadth)
        column = lax.broadcasted_iota(jnp.int32, wide.shape, 1) // RANK
        blocks.append(jnp.where(row == column, wide, 0.0))
        breadth //= 2
    whole = jnp.concatenate(blocks + [bases[-1]], axis=1)
    turned = whole.T
    bb_ref[:, :ROWS] = whole
    bb_ref[:, ROWS:] = turned
    x = x_ref[...]
    everything = mul(
        turned, jnp.concatenate([x, bases[-1], jnp.zeros((ROWS, 32), jnp.float32)], axis=1)
    )
    write_rim(up_ref, everything[:COEF, :NRHS], x[ROWS - RIM :])
    write_rim(down_ref, everything[:COEF, :NRHS], x[:RIM])
    up_ref[RIM_ROWS:, :] = everything[COEF:]
    down_ref[RIM_ROWS:, :] = everything[COEF:]


def record_kernel(me_ref, own_ref, before_ref, after_ref, pair_ref, tile_ref, out_ref, gram_ref):
    core = me_ref[0] % 2
    other = jnp.where(core == 0, after_ref[RIM_ROWS:, :], before_ref[RIM_ROWS:, :])
    both = own_ref[RIM_ROWS:, :] + other
    out_ref[0, 0:8, :] = pack(pick_half(both, core))
    out_ref[0, 8:16, :] = pair_ref[...]
    out_ref[0, 16:48, :] = tile_ref[...]
    gram_ref[...] = both[:, NRHS : NRHS + RANK]


def near_kernel(me_ref, count_ref, partner_ref, block_ref, band_ref, total):
    total[...] = jnp.zeros_like(total)
    first = me_ref[0] * L_DEV
    for t in range(L_DEV):
        for s in range(NEARP):

            @pl.when(s < count_ref[t])
            def _(t=t, s=s):
                at = jnp.clip(partner_ref[t, s] - (first + t) + NW, 0, 2 * NW)
                rows = (s * L_DEV + t) * LEAF
                total[t, at] += block_ref[rows : rows + LEAF, :]

    for t in range(L_DEV):
        band_ref[t * LEAF : (t + 1) * LEAF, :] = jnp.concatenate(
            [total[t, k] for k in range(2 * NW + 1)], axis=1
        )


def couple_kernel(count_ref, block_ref, out_ref):
    for r in range(CPD):
        parts = []
        for s in range(FARP):
            at = (r * FARP + s) * RANK
            parts.append(jnp.where(s < count_ref[r], block_ref[at : at + RANK, :], 0.0))
        out_ref[r * RANK : (r + 1) * RANK, :] = jnp.concatenate(parts, axis=1)


def local_kernel(
    me_ref, far_ref, band_ref, couple_ref, bb_ref, x_ref, up_ref, before_ref, after_ref,
    y_ref, share_ref, xe, ce, far_pick, far_sum
):
    xe[0:RIM, :] = read_rows(before_ref)
    xe[RIM : RIM + ROWS, :] = x_ref[...]
    xe[RIM + ROWS :, :] = read_rows(after_ref)
    ce[0:COEF, :] = read_coefs(before_ref)
    ce[COEF : 2 * COEF, :] = read_coefs(up_ref)
    ce[2 * COEF :, :] = read_coefs(after_ref)
    me = me_ref[0]
    r = 0
    breadth = L_DEV
    while breadth >= 1:
        offset = 2 * L_DEV - 2 * breadth
        for _ in range(breadth):
            for s in range(FARP):
                along = jnp.clip(far_ref[s, r] - (me - 1) * breadth, 0, 3 * breadth - 1)
                place = along // breadth * CPD + offset + along % breadth
                at = pl.multiple_of(place * RANK, RANK)
                far_pick[r, s * RANK : (s + 1) * RANK, :] = ce[pl.ds(at, RANK), :]
            r += 1
        breadth //= 2
    for r in range(CPD):
        rows = slice(r * RANK, (r + 1) * RANK)
        far_sum[rows, :] = mul(couple_ref[rows, :], far_pick[r])
    spread = mul(bb_ref[:, :COEF], far_sum[...])
    for t in range(L_DEV):
        rows = slice(t * LEAF, (t + 1) * LEAF)
        window = xe[t * LEAF : (t + 2 * NW + 1) * LEAF, :]
        y_ref[rows, :] = spread[rows] + mul(band_ref[rows, :], window)
    share_ref[...] = mul(bb_ref[COEF:, ROWS:], y_ref[...])


def links_kernel(me_ref, u_ref, q_ref):
    row = lax.broadcasted_iota(jnp.int32, (128, 128), 0)
    column = lax.broadcasted_iota(jnp.int32, (128, 128), 1)
    same = row // RANK == column // RANK
    product = None
    for k, m in enumerate(LEVELS[:-1]):
        ancestor = first_of(m) + me_ref[0] // (DEVICES // m)
        link = u_ref[pl.ds(pl.multiple_of(ancestor * RANK, RANK), RANK), :]
        product = link if product is None else mul(product, link)
        wide = jnp.concatenate([product.T] * 4, axis=1)
        tall = jnp.concatenate([wide] * 4, axis=0)
        q_ref[k] = jnp.where(same, tall, 0.0)


def fold_kernel(
    me_ref, a0, a1, a2, a3, b0, b1, b2, b3, q_ref, u_ref, _, w_ref, t_ref, total, ready, turned
):
    first, second = (a0, a1, a2, a3), (b0, b1, b2, b3)
    me = me_ref[0]
    per = CHIPS // 4
    for k, piece in enumerate(first):
        t_ref[k * per * 8 : (k + 1) * per * 8, :] = piece[:, 0:8, :].reshape(per * 8, 128)
    pairs = jnp.concatenate([piece[:, 8, :] for piece in first], axis=0)
    swapped = jnp.concatenate(
        [pairs[per * x + 8 * y : per * x + 8 * y + 8] for y in range(4) for x in range(4)], axis=0
    )
    pairs, swapped = pairs.T, swapped.T
    mask = []
    for j in range(HOLD):
        table = pairs if j == 0 else swapped
        target = table[j : j + 1, :].astype(jnp.int32)
        source = table[HOLD + j : HOLD + j + 1, :].astype(jnp.int32)
        wanted = target < 0
        for m in LEVELS:
            wanted = wanted | (target == first_of(m) + me // (DEVICES // m))
        source = jnp.where(wanted, source, -1)
        row = lax.broadcasted_iota(jnp.int32, (256, CHIPS), 0)
        mask.append(jnp.where(row == source, 1.0, 0.0).astype(jnp.bfloat16))
    mask = jnp.concatenate(mask, axis=1)
    for r in range(8):
        rows = jnp.concatenate(
            [piece[:, 16 + r, :] for piece in first]
            + [piece[:, 8 * j + r, :] for j in range(HOLD - 1) for piece in second],
            axis=0,
        )
        high, low = split(rows)
        both = dot(mask, jnp.concatenate([high, low], axis=1))
        total[:, r, :] = both[:, :128] + both[:, 128:]
    direct = {}
    for k, m in enumerate(LEVELS[1:]):
        o = first_of(m)
        packed = mul(total[o : o + m].reshape(m * 8, 128), q_ref[k])
        for u in range(m):
            direct[m, u] = packed[8 * u : 8 * u + 8]
    above = [unpack(direct[2, u]) for u in range(2)]
    for m in (4, 8, 16, 32, 64, 128):
        o = first_of(m)
        level = []
        for q in range(m // 2):
            high, low = split(above[q])
            stack = jnp.concatenate([high, high, low], axis=0)
            at = (o + 2 * q) * RANK
            left, rest = split(u_ref[at : at + 2 * RANK, :])
            grown = dot(jnp.concatenate([left, rest, left], axis=1), stack)
            for i in range(2):
                part = grown[i * RANK : (i + 1) * RANK]
                if m < 128:
                    level.append(unpack(direct[m, 2 * q + i]) + part)
                else:
                    ready[2 * q + i] = total[2 * q + i] + pack(part)
        above = level
    for i in range(CHIPS):
        turned[8 * i : 8 * i + 8, :] = ready[gathered_chip(me, i)]
    w_ref[...] = turned[...].T


def diagonal(z):
    return sum(z[g * RANK : (g + 1) * RANK, g * HALF : (g + 1) * HALF] for g in range(4))


def middle_kernel(me_ref, w0_ref, w1_ref, t_ref, gram_ref, s0_ref, s1_ref, w_ref, ud_ref, next_ref):
    w = w0_ref[...] + w1_ref[...]
    w_ref[...] = w
    ud = diagonal(mul(w, t_ref[...]))
    ud_ref[...] = ud
    share = pick_half(s0_ref[...] + s1_ref[...], me_ref[0] % 2)
    next_ref[0] = pack(share + mul(gram_ref[...], ud))


def last_kernel(w_ref, p0, p1, p2, p3, _, ud_ref):
    t = jnp.concatenate([p[...].reshape(CHIPS * 2, 128) for p in (p0, p1, p2, p3)], axis=0)
    ud_ref[...] = diagonal(mul(w_ref[...], t))


def finish_up_kernel(me_ref, y_ref, own_ref, other_ref, bb_ref, out_ref, up_ref, down_ref):
    ud = both_halves(own_ref[...], other_ref[...], me_ref[0] % 2)
    out = y_ref[...] + mul(bb_ref[:, COEF:ROWS], ud)
    out_ref[...] = out
    coefs = mul(bb_ref[:COEF, ROWS:], out)
    write_rim(up_ref, coefs, out[ROWS - RIM :])
    write_rim(down_ref, coefs, out[:RIM])


def finish_kernel(me_ref, y_ref, own_ref, other_ref, bb_ref, out_ref):
    ud = both_halves(own_ref[...], other_ref[...], me_ref[0] % 2)
    out_ref[...] = y_ref[...] + mul(bb_ref[:, COEF:ROWS], ud)


def body(
    block_in, leaf_basis, transfer, upper_transfer, near_count, near_partner, near_block,
    far_count, far_partner, coupling, upper_pair, upper_block
):
    me = lax.axis_index("dev").reshape(1)

    vectors = block_in.reshape(ROWS, NRHS)
    bb, up, down = call(
        basis_kernel,
        [f32(ROWS, 2 * ROWS), f32(RIM_ROWS + RANK, 128), f32(RIM_ROWS + RANK, 128)],
        [leaf_basis.reshape(ROWS, RANK), transfer.reshape(COEF, RANK), vectors],
        flops=100_000_000,
    )
    before, after = neighbours(up, down)

    tiles = upper_block.reshape(HOLD, RANK, 4, 8).transpose(0, 3, 2, 1).reshape(HOLD * 8, 128)
    pairs = jnp.pad(
        upper_pair.astype(jnp.float32).T.reshape(1, 2 * HOLD), ((0, 7), (0, 128 - 2 * HOLD))
    )
    record, gram = call(
        record_kernel,
        [f32(1, 48, 128), f32(RANK, RANK)],
        [me, up, before, after, pairs, tiles],
        smem=1,
    )

    (couple,) = call(
        couple_kernel,
        [f32(COEF, FARP * RANK)],
        [far_count, coupling.reshape(CPD * FARP * RANK, RANK)],
        smem=1,
    )
    links = upper_transfer.reshape(UPE * RANK, RANK)
    (q,) = call(links_kernel, [f32(6, 128, 128)], [me, links], smem=1)
    record = gather_z(record, between=[couple], after=[q])

    def local(x, up, before, after):
        return call(
            local_kernel,
            [f32(ROWS, NRHS), f32(RANK, NRHS)],
            [me, far_partner.T, band, couple, bb, x, up, before, after],
            scratch=[
                pltpu.VMEM((ROWS + 2 * RIM, NRHS), jnp.float32),
                pltpu.VMEM((3 * COEF, NRHS), jnp.float32),
                pltpu.VMEM((CPD, FARP * RANK, NRHS), jnp.float32),
                pltpu.VMEM((COEF, NRHS), jnp.float32),
            ],
            smem=2,
            flops=300_000_000,
            size=4_000_000,
        )

    def halves(part, last, other):
        both = join([part, lax.ppermute(part, "dev", ring(*last, 2))])
        parts = spread(both, other)
        return join([p[:8] for p in parts]), join([p[8:] for p in parts])

    def ends(near, opposite, last):
        return [
            near,
            lax.ppermute(near, "dev", ring(*last, 1)),
            opposite,
            lax.ppermute(near, "dev", ring(*last, 3)),
        ]

    half_a, opposite_a = halves(record[:, :24], X_AXIS, Y_AXIS)
    half_b, opposite_b = halves(record[:, 24:], Y_AXIS, X_AXIS)
    near_rows = near_block.transpose(1, 0, 2).reshape(NEARP * L_DEV * LEAF, LEAF)
    half_a, half_b, near_rows = lax.optimization_barrier((half_a, half_b, near_rows))
    pieces = ends(half_a, opposite_a, X_AXIS) + ends(half_b, opposite_b, Y_AXIS)

    (band,) = call(
        near_kernel,
        [f32(ROWS, (2 * NW + 1) * LEAF)],
        [me, near_count, near_partner, near_rows],
        scratch=[pltpu.VMEM((L_DEV, 2 * NW + 1, LEAF, LEAF), jnp.float32)],
        smem=3,
    )
    near_first, share = local(vectors, up, before, after)
    share_other = other_core(share)

    w_own, first_coefs = call(
        fold_kernel,
        [f32(128, CHIPS * 8), f32(CHIPS * 8, 128)],
        [me, *pieces, q, links, share],
        scratch=[
            pltpu.VMEM((256, 8, 128), jnp.float32),
            pltpu.VMEM((CHIPS, 8, 128), jnp.float32),
            pltpu.VMEM((CHIPS * 8, 128), jnp.float32),
        ],
        smem=1,
        flops=100_000_000,
        room=16,
    )
    w, ud, second_record = call(
        middle_kernel,
        [f32(128, CHIPS * 8), f32(RANK, HALF), f32(1, 8, 128)],
        [me, w_own, other_core(w_own), first_coefs, gram, share, share_other],
        smem=1,
        flops=100_000_000,
    )
    ud_other = other_core(ud)
    first_rows, up, down = call(
        finish_up_kernel,
        [f32(ROWS, NRHS), f32(RIM_ROWS, 128), f32(RIM_ROWS, 128)],
        [me, near_first, ud, ud_other, bb],
        smem=1,
        flops=100_000_000,
    )
    second_record = gather_z(second_record, between=[ud_other], after=[up])
    up, down, second_record = lax.optimization_barrier((up, down, second_record))
    before, after = neighbours(up, down)
    second_pieces = spread(join(spread(second_record, Y_AXIS)), X_AXIS)
    near_second, share = local(first_rows, up, before, after)
    (ud,) = call(last_kernel, [f32(RANK, HALF)], [w, *second_pieces, share], flops=100_000_000)
    (second_rows,) = call(
        finish_kernel, [f32(ROWS, NRHS)], [me, near_second, ud, other_core(ud), bb], smem=1
    )
    return (
        first_rows.reshape(L_DEV, LEAF * NRHS),
        second_rows.reshape(L_DEV, LEAF * NRHS),
    )


def solution(mesh):
    in_specs = (
        P("dev", None),
        P("dev", None),
        P("dev", None),
        P(),
        P("dev"),
        P("dev", None),
        P("dev", None, None),
        P("dev"),
        P("dev", None),
        P("dev", None, None),
        P("dev", None),
        P("dev", None),
    )
    out_specs = (P("dev", None), P("dev", None))
    return jax.shard_map(body, mesh=mesh, in_specs=in_specs, out_specs=out_specs, check_vma=False)
```
